256 devices in a mesh: row: 8 (over y, z_hi), col: 32 (over x, z_lo, core).
Axes of the slice: x: 4, y: 4, z: 8 (z_hi: 2, z_lo: 4; z = z_hi * 4 + z_lo), core: 2. Of those that a mesh axis runs over, the one named last changes fastest.
Arguments:
- latent: float32 [4, 1024, 1024], P(None, 'col', 'row')
- row_offset: int32 [1], replicated, may hold values from 1 to 127
- col_offset: int32 [1], replicated, may hold values from 1 to 31
- timestep: int32 [1], replicated, may hold values from 0 to 999
- w_in: bfloat16 [9, 320, 4], replicated, may hold values from -1 to 1
- norm_gain: float32 [320], replicated, may hold values from 0.1 to 1.9
- norm_shift: float32 [320], replicated, may hold values from -3 to 3
- w_conv: bfloat16 [9, 320, 320], P(None, 'col'), may hold values from -0.109375 to 0.109375
- w_time1: bfloat16 [320, 1280], P(None, 'col'), may hold values from -0.3125 to 0.3125
- w_time2: bfloat16 [1280, 1280], P('col'), may hold values from -0.15625 to 0.15625
- w_time3: bfloat16 [1280, 320], P(None, 'col'), may hold values from -0.15625 to 0.15625
Outputs:
- conv_out: bfloat16 [320, 1024, 1024], P(None, 'col', 'row')
The draws below stay inside these ranges and needn't reach their ends.
All inputs are finite; a program needn't handle non-finite values.
Results may differ from the reference program's by a relative error of at most 0.0057.
Values may be sent and summed in bfloat16 or wider, within the bound.
No kernel may reach another device: no remote copies, remote signals or barrier semaphores. Data moves between devices by JAX's collectives and lax.ppermute only.
A program may use at most 128 MiB of HBM per device.

```python
import jax
import jax.numpy as jnp
from jax import lax

CH = 320
GROUPS = 32
TEMB = 1280
LAT_C = 4
WIN = 128
TW = 32
HEIGHT = 1024
WIDTH = 1024


def draw_latent(key, part):
    key = jax.random.fold_in(key, 11)
    noise_key = jax.random.fold_in(key, 0)
    row_pos = jnp.arange(HEIGHT, dtype=jnp.float32) / jnp.float32(max(HEIGHT - 1, 1))
    col_pos = jnp.arange(WIDTH, dtype=jnp.float32) / jnp.float32(max(WIDTH - 1, 1))
    values = jax.random.normal(noise_key, (LAT_C, WIDTH, HEIGHT), jnp.float32)
    scale = (3.0 ** col_pos)[:, None] * (3.0 ** row_pos)[None, :] / 3.0
    return (values * scale[None, :, :]).astype(jnp.float32)


def block_levels(own_key, extent, cuts, smallest, largest):
    gain = 1.0
    for axis_at, parts in cuts:
        draws = jax.random.uniform(jax.random.fold_in(jax.random.fold_in(own_key, 6), axis_at), (parts,), jnp.float32, smallest / len(cuts), largest / len(cuts))
        gain = gain * jnp.repeat(jnp.exp(draws), extent[axis_at] // parts).reshape((-1,) + (1,) * (len(extent) - 1 - axis_at))
    return gain


def bell_draw(rng, extent, width, most, pieces=(), kind=jnp.bfloat16):
    drawn = jax.random.normal(rng, extent, jnp.float32) * width
    if len(pieces) > 0:
        drawn = block_levels(rng, extent, pieces, -0.22, 0.18) * drawn
    return jnp.clip(drawn, min=-most, max=most).astype(kind)


def setup_inputs(seed: int = 0) -> dict:
    key_of = jax.random.split(jax.random.key(seed), 12)
    return {
        "latent": draw_latent(jax.random.fold_in(key_of[11], 71), 0),
        "row_offset": jax.random.randint(key_of[1], (1,), 1, WIN).astype(jnp.int32),
        "col_offset": jax.random.randint(key_of[2], (1,), 1, TW).astype(jnp.int32),
        "timestep": jax.random.randint(key_of[3], (1,), 0, 1000).astype(jnp.int32),
        "w_in": bell_draw(key_of[4], (9, CH, LAT_C), (9 * LAT_C) ** -0.5, 1.0),
        "norm_gain": jnp.clip(1.0 + 0.18 * jax.random.normal(key_of[5], (CH,), jnp.float32), 0.1, 1.9),
        "norm_shift": bell_draw(key_of[6], (CH,), 0.5, 3.0, (), jnp.float32),
        "w_conv": bell_draw(key_of[7], (9, CH, CH), (9 * CH) ** -0.5, 0.109375, ((1, 32),)),
        "w_time1": bell_draw(key_of[8], (CH, TEMB), CH ** -0.5, 0.3125, ((1, 32),)),
        "w_time2": bell_draw(key_of[9], (TEMB, TEMB), TEMB ** -0.5, 0.15625, ((0, 32),)),
        "w_time3": bell_draw(key_of[10], (TEMB, CH), TEMB ** -0.5, 0.15625, ((1, 32),)),
    }


def sinusoid(timestep):
    half = CH // 2
    freq = jnp.exp(-jnp.log(jnp.float32(10000.0)) * jnp.arange(half, dtype=jnp.float32) / jnp.float32(half))
    angle = timestep[0].astype(jnp.float32) * freq
    return jnp.concatenate([jnp.cos(angle), jnp.sin(angle)])

def convolve(weights, image):
    chans, cols, rows = image.shape
    padded = jnp.pad(image, ((0, 0), (1, 1), (1, 1)))
    total = jnp.zeros((weights.shape[1], cols * rows), jnp.float32)
    for tap_a in range(3):
        for tap_b in range(3):
            window = padded[:, tap_b:tap_b + cols, tap_a:tap_a + rows].reshape(chans, cols * rows)
            total = total + jnp.dot(weights[3 * tap_a + tap_b], window, preferred_element_type=jnp.float32)
    return total

def window_step(window, w_in, norm_gain, norm_shift, w_conv, tvec):
    feat = convolve(w_in, window)
    grouped = feat.reshape(GROUPS, -1)
    mean = lax.optimization_barrier(jnp.mean(grouped, axis=1, keepdims=True))
    var = lax.optimization_barrier(jnp.mean((grouped - mean) ** 2, axis=1, keepdims=True))
    normed = ((grouped - mean) / jnp.sqrt(var + 1e-05)).reshape(CH, -1) * norm_gain[:, None] + norm_shift[:, None]
    hidden = jax.nn.silu(normed).astype(jnp.bfloat16).reshape(CH, WIN, WIN)
    conv = convolve(w_conv, hidden) + tvec[:, None]
    return conv.astype(jnp.bfloat16).reshape(CH, WIN, WIN)

def reference(latent, row_offset, col_offset, timestep, w_in, norm_gain, norm_shift, w_conv, w_time1, w_time2, w_time3):
    moved = jnp.roll(latent, (-col_offset[0], -row_offset[0]), axis=(1, 2)).astype(jnp.bfloat16)
    moved = jnp.roll(moved, -(WIN // 2), axis=1)
    across = WIDTH // WIN
    down = HEIGHT // WIN
    windows = moved.reshape(LAT_C, across, WIN, down, WIN).transpose(1, 3, 0, 2, 4).reshape(across * down, LAT_C, WIN, WIN)
    emb = sinusoid(timestep)
    first = jnp.dot(emb, w_time1.astype(jnp.float32), precision=lax.Precision.HIGHEST)
    e_one = jax.nn.silu(first).astype(jnp.bfloat16)
    e_two = jnp.dot(e_one, w_time2, preferred_element_type=jnp.float32)
    s_two = jax.nn.silu(e_two).astype(jnp.bfloat16)
    tvec = jnp.dot(s_two, w_time3, preferred_element_type=jnp.float32)

    def one_window(window):
        return window_step(window, w_in, norm_gain, norm_shift, w_conv, tvec)
    results = lax.map(one_window, windows)
    whole = results.reshape(across, down, CH, WIN, WIN).transpose(2, 0, 3, 1, 4).reshape(CH, WIDTH, HEIGHT)
    return jnp.roll(whole, WIN // 2, axis=1)
```

```python
import jax
import jax.numpy as jnp
from jax import lax
from jax.experimental import pallas as pl
from jax.experimental.pallas import tpu as pltpu
from jax.sharding import PartitionSpec as P

WIN = 128
LANES = 128
EDGE = 2
HIGH = lax.Precision.HIGHEST
ROWS = 8
TAPS = 9


def features_kernel(phase_ref, window_ref, w_ref, gain_ref, shift_ref, hidden_ref, shifted):
    chans = w_ref.shape[0]
    tile = window_ref.shape[2]
    width = tile // LANES
    lat = window_ref.shape[1]
    span = WIN * LANES
    total = span + 2 * EDGE * LANES
    lane = lax.broadcasted_iota(jnp.int32, (ROWS, tile), 1) % LANES
    zeros_edge = jnp.zeros((ROWS, EDGE * LANES), jnp.float32)
    for a in range(3):
        shifted[a, :, 0 : EDGE * LANES] = zeros_edge
        shifted[a, :, total - EDGE * LANES : total] = zeros_edge
    for part in range(window_ref.shape[0]):
        cells = window_ref[part].astype(jnp.float32)
        cells = jnp.concatenate([cells, jnp.zeros((ROWS - lat, tile), jnp.float32)], axis=0)
        at = EDGE * LANES + part * tile
        shifted[0, :, at : at + tile] = jnp.where(lane == 0, 0.0, pltpu.roll(cells, 1, 1))
        shifted[1, :, at : at + tile] = cells
        shifted[2, :, at : at + tile] = jnp.where(
            lane == LANES - 1, 0.0, pltpu.roll(cells, tile - 1, 1)
        )

    def tap_views(start, size):
        return [
            shifted[a, :, pl.ds(start + (b - 1) * LANES, size)]
            for a in range(3)
            for b in range(3)
        ]

    count = float(span)
    sums = [jnp.sum(v, axis=1, keepdims=True) for v in tap_views(EDGE * LANES, span)]
    xbar = jnp.concatenate(sums, axis=0) * (1.0 / count)

    def gram_step(step, carry):
        same, cross = carry
        start = pl.multiple_of(EDGE * LANES + step * 2048, LANES)
        cells = jnp.concatenate(
            [
                shifted[a, :, pl.ds(pl.multiple_of(start + (b - 1) * LANES, LANES), 2048)]
                for a in range(3)
                for b in range(3)
            ],
            axis=0,
        )
        centred = cells - xbar
        high = centred.astype(jnp.bfloat16)
        low = (centred - high.astype(jnp.float32)).astype(jnp.bfloat16)
        dims = (((1,), (1,)), ((), ()))
        same = same + lax.dot_general(high, high, dims, preferred_element_type=jnp.float32)
        cross = cross + lax.dot_general(high, low, dims, preferred_element_type=jnp.float32)
        return same, cross

    depth = TAPS * ROWS
    blank = jnp.zeros((depth, depth), jnp.float32)
    same, cross = lax.fori_loop(0, span // 2048, gram_step, (blank, blank))
    spread = (same + 2.0 * cross) * (1.0 / count)
    w_bf = w_ref[...]
    w = w_bf.astype(jnp.float32)
    chan_mean = jnp.dot(
        w, jnp.broadcast_to(xbar, (depth, LANES)), precision=HIGH, preferred_element_type=jnp.float32
    )
    quad = jnp.dot(w, spread, precision=HIGH, preferred_element_type=jnp.float32) * w
    chan_var = jnp.sum(quad, axis=1, keepdims=True)
    of_row = (lax.broadcasted_iota(jnp.int32, (chans, chans), 0) * 6554) >> 16
    of_col = (lax.broadcasted_iota(jnp.int32, (chans, chans), 1) * 6554) >> 16
    member = (of_row == of_col).astype(jnp.float32)
    mean = jnp.dot(member, chan_mean, precision=HIGH, preferred_element_type=jnp.float32) * 0.1
    off = chan_mean - mean
    var = jnp.dot(member, chan_var + off * off, precision=HIGH, preferred_element_type=jnp.float32) * 0.1
    scale = 0.5 * gain_ref[...] / jnp.sqrt(var + 1e-05)
    base = 0.5 * shift_ref[...] - mean * scale

    phase = phase_ref[0]
    first, last = phase == 0, phase == 3
    scale2 = jnp.concatenate([scale, scale], axis=1)
    base2 = jnp.concatenate([base, base], axis=1)
    pairs = (width + 2) // 2
    for pair in range(pairs):
        start = phase * tile + pair * 2 * LANES
        cells = jnp.concatenate(
            [
                shifted[a, :, pl.ds(pl.multiple_of(start + b * LANES, LANES), 2 * LANES)]
                for a in range(3)
                for b in range(3)
            ],
            axis=0,
        ).astype(jnp.bfloat16)
        feat = jnp.dot(w_bf, cells, preferred_element_type=jnp.float32)
        half = feat * scale2 + base2
        act = half * jnp.tanh(half) + half
        if pair == 0:
            keep = jnp.where(first, 0.0, 1.0)
            act = jnp.concatenate([jnp.where(first, 0.0, act[:, :LANES]), act[:, LANES:]], axis=1)
        if pair == pairs - 1:
            act = jnp.concatenate([act[:, :LANES], jnp.where(last, 0.0, act[:, LANES:])], axis=1)
        hidden_ref[:, pair * 2 * LANES : (pair + 1) * 2 * LANES] = act.astype(jnp.bfloat16)


def features(phase, window, w_taps, gain, shift):
    parts, lat, tile = window.shape
    chans = w_taps.shape[0]
    width = tile // LANES
    return pl.pallas_call(
        features_kernel,
        out_shape=jax.ShapeDtypeStruct((chans, (width + 2) * LANES), jnp.bfloat16),
        in_specs=[pl.BlockSpec(memory_space=pltpu.SMEM)]
        + [pl.BlockSpec(memory_space=pltpu.VMEM)] * 4,
        out_specs=pl.BlockSpec(memory_space=pltpu.VMEM),
        scratch_shapes=[pltpu.VMEM((3, ROWS, (WIN + 2 * EDGE) * LANES), jnp.float32)],
        compiler_params=pltpu.CompilerParams(vmem_limit_bytes=40 * 2**20),
        name="features",
    )(phase, window, w_taps, gain, shift)


COLS = 4
HALF_COLS = 16
KPAD = 512


def conv_kernel(place_ref, hidden_ref, s2_ref, *rest):
    blocks = rest[:8]
    out_ref, wide = rest[8], rest[9]
    core, xpos = place_ref[0], place_ref[1]
    step = pl.program_id(0)
    chans = hidden_ref.shape[0]
    half = chans // 2
    own = pl.multiple_of(core * half, 16)
    other = pl.multiple_of((1 - core) * half, 16)
    n = COLS * LANES
    lane = lax.broadcasted_iota(jnp.int32, (80, n), 1) % LANES
    tvecs = []
    for k in range(4):
        t_own = blocks[k][0:80, 3 * KPAD :].astype(jnp.float32) * s2_ref[0:1, :]
        t_oth = blocks[4 + k][0:80, 3 * KPAD :].astype(jnp.float32) * s2_ref[1:2, :]
        tvecs.append(jnp.sum(t_own + t_oth, axis=1, keepdims=True))

    def one(tile, _):
        col = step * HALF_COLS + tile * COLS
        right = []
        for rows in (own, other):
            for b in range(3):
                at = pl.multiple_of((col + b) * LANES, LANES)
                right.append(hidden_ref[pl.ds(rows, half), pl.ds(at, n)])
            right.append(right[-1][0 : KPAD - 3 * half])
        right = jnp.concatenate(right, axis=0)
        left = jnp.concatenate(
            [
                jnp.concatenate(
                    [
                        blocks[k][0:80, a * KPAD : (a + 1) * KPAD],
                        blocks[4 + k][0:80, a * KPAD : (a + 1) * KPAD],
                    ],
                    axis=1,
                )
                for k in range(4)
                for a in range(3)
            ],
            axis=0,
        )
        prod = jnp.dot(left, right, preferred_element_type=jnp.float32)
        for k in range(4):
            low, mid, high = (prod[(3 * k + a) * 80 : (3 * k + a + 1) * 80] for a in range(3))
            done = (
                mid
                + jnp.where(lane == 0, 0.0, pltpu.roll(low, 1, 1))
                + jnp.where(lane == LANES - 1, 0.0, pltpu.roll(high, n - 1, 1))
                + tvecs[k]
            )
            chan = (xpos + (0, 1, 3, 2)[k]) % 4 * 80
            for j in range(COLS):
                first = chan * HALF_COLS + tile * COLS + j
                wide[pl.ds(first, 80, stride=HALF_COLS), :] = done[:, j * LANES : (j + 1) * LANES]
        return 0

    lax.fori_loop(0, HALF_COLS // COLS, one, 0)
    out_ref[...] = wide[...].reshape(chans, HALF_COLS, LANES).astype(jnp.bfloat16)


def conv(place, hidden, s_two, blocks):
    chans, padded = hidden.shape
    width = padded // LANES - 2
    whole = lambda *shape: pl.BlockSpec(shape, lambda i: (0,) * len(shape))
    return pl.pallas_call(
        conv_kernel,
        grid=(width // HALF_COLS,),
        out_shape=jax.ShapeDtypeStruct((chans, width, LANES), jnp.bfloat16),
        in_specs=[
            pl.BlockSpec(memory_space=pltpu.SMEM),
            whole(*hidden.shape),
            whole(*s_two.shape),
        ]
        + [whole(*b.shape) for b in blocks],
        out_specs=pl.BlockSpec((chans, HALF_COLS, LANES), lambda i: (0, i, 0)),
        scratch_shapes=[pltpu.VMEM((chans * HALF_COLS, LANES), jnp.float32)],
        compiler_params=pltpu.CompilerParams(vmem_limit_bytes=56 * 2**20),
        name="convolve",
    )(place, hidden, s_two, *blocks)


def pairs_of(move):
    pairs = []
    for row in range(8):
        for col in range(32):
            y, z_hi, x, z_lo, core = row // 2, row % 2, col // 8, col // 2 % 4, col % 2
            z = z_hi * 4 + z_lo
            y, z, x, core = move(y, z, x, core)
            y, z, x = y % 4, z % 8, x % 4
            pairs.append((row * 32 + col, (y * 2 + z // 4) * 32 + x * 8 + z % 4 * 2 + core))
    return pairs


def send(value, move):
    return lax.ppermute(value, ("row", "col"), pairs_of(move))


def fetch_grid(value, rows, cols):
    pairs = [
        ((r + rows) % 8 * 32 + (c + cols) % 32, r * 32 + c) for r in range(8) for c in range(32)
    ]
    return lax.ppermute(value, ("row", "col"), pairs)


def swap_core(value):
    return send(value, lambda y, z, x, core: (y, z, x, 1 - core))


def from_z(value, steps):
    return send(value, lambda y, z, x, core: (y, z - steps, x, core))


def from_x(value, steps):
    return send(value, lambda y, z, x, core: (y, z, x - steps, core))


WINDOW_GROUPS = [[r * 32 + (4 * p + 2 + k) % 32 for k in range(4)] for r in range(8) for p in range(8)]


def sinusoid(timestep, chans):
    half = chans // 2
    freq = jnp.exp(
        -jnp.log(jnp.float32(10000.0)) * jnp.arange(half, dtype=jnp.float32) / jnp.float32(half)
    )
    angle = timestep[0].astype(jnp.float32) * freq
    return jnp.concatenate([jnp.cos(angle), jnp.sin(angle)])


def split_rows(value, width, rows):
    high = lax.reduce_precision(value, 8, 7)
    low = lax.reduce_precision(value - high, 8, 7)
    both = jnp.stack([high, low]).astype(jnp.bfloat16)
    return jnp.pad(both, ((0, rows - 2), (0, width - value.shape[0])))


def join_rows(rows, size):
    rows = rows[:, :size].astype(jnp.float32)
    return rows[0] + rows[1]


def body(
    latent,
    row_offset,
    col_offset,
    timestep,
    w_in,
    norm_gain,
    norm_shift,
    w_conv,
    w_time1,
    w_time2,
    w_time3,
):
    chans, lat = w_in.shape[1:]
    width, height = latent.shape[1:]
    temb = w_time2.shape[1]
    shard = w_conv.shape[1]
    col = lax.axis_index("col")
    core, z_lo, x = col % 2, col // 2 % 4, col // 8
    phase = (col + 30) % 4

    own = latent.astype(jnp.bfloat16)
    below, beside, corner = fetch_grid(own, 1, 0), fetch_grid(own, 0, 1), fetch_grid(own, 1, 1)

    emb = sinusoid(timestep, chans)
    first = jnp.dot(emb, w_time1.astype(jnp.float32), precision=lax.Precision.HIGHEST)
    e_one = jax.nn.silu(first).astype(jnp.bfloat16)
    e_two = jnp.dot(e_one, w_time2, preferred_element_type=jnp.float32)

    taps = w_conv.reshape(3, 3, shard, 2, chans // 2).transpose(3, 2, 0, 1, 4)
    taps = taps.reshape(2, shard, 3, 3 * (chans // 2))
    taps = jnp.pad(taps, ((0, 0), (0, 0), (0, 0), (0, KPAD - 3 * (chans // 2)))).reshape(2, shard, 3 * KPAD)
    third = w_time3.T.reshape(shard, 2, temb // 2).transpose(1, 0, 2)
    halves = jnp.concatenate([taps, third], axis=2)
    wide = halves.shape[2]
    mine = lax.dynamic_index_in_dim(halves, core, 0, keepdims=False)
    theirs = lax.dynamic_index_in_dim(halves, 1 - core, 0, keepdims=False)
    got = swap_core(jnp.concatenate([theirs, split_rows(e_two, wide, 2)]))
    e_two = e_two + join_rows(got[shard:], temb)
    pair = jnp.where(
        core == 0,
        jnp.concatenate([mine, got[:shard]]),
        jnp.concatenate([got[:shard], mine]),
    )
    zrow = jnp.concatenate([pair, split_rows(e_two, wide, 2)])
    near = [zrow, from_z(zrow, 1), from_z(zrow, 2), from_z(zrow, -1)]
    e_two = sum([join_rows(v[2 * shard :], temb) for v in near[1:]], e_two)
    ring = jnp.concatenate([v[: 2 * shard] for v in near + near])
    block = lax.dynamic_slice_in_dim(ring, (4 - z_lo) % 4 * 2 * shard, 8 * shard, 0)
    block = jnp.concatenate([block, split_rows(e_two, wide, 8)])
    after, before = from_x(block, 1), from_x(block, -1)
    cut = 48
    across = jnp.concatenate([from_x(after[:cut], 1), from_x(before[cut:], -1)])
    blocks = [block, after, before, across]
    e_two = sum([join_rows(v[8 * shard : 8 * shard + 2], temb) for v in blocks[1:]], e_two)
    blocks = blocks + [swap_core(v) for v in blocks]
    s_two = jax.nn.silu(e_two).astype(jnp.bfloat16).astype(jnp.float32).reshape(2, temb // 2)
    s_two = jnp.where(core == 0, s_two, s_two[::-1])

    grid = jnp.concatenate(
        [jnp.concatenate([own, below], axis=2), jnp.concatenate([beside, corner], axis=2)], axis=1
    )
    moved = lax.dynamic_slice(grid, (0, col_offset[0], row_offset[0]), (lat, width, height))
    window = lax.all_gather(
        moved.reshape(lat, width * height), ("row", "col"), axis_index_groups=WINDOW_GROUPS, axis=0
    )
    w_taps = jnp.pad(w_in.transpose(1, 0, 2), ((0, 0), (0, 0), (0, ROWS - lat))).reshape(chans, TAPS * ROWS)
    wide_gain = jnp.broadcast_to(norm_gain[:, None], (chans, LANES))
    wide_shift = jnp.broadcast_to(norm_shift[:, None], (chans, LANES))
    hidden = features(phase[None], window, w_taps, wide_gain, wide_shift)
    return conv(jnp.stack([core, x]), hidden, s_two, blocks)


def solution(mesh):
    return jax.shard_map(
        body,
        mesh=mesh,
        in_specs=(
            P(None, "col", "row"),
            P(),
            P(),
            P(),
            P(),
            P(),
            P(),
            P(None, "col", None),
            P(None, "col"),
            P("col", None),
            P(None, "col"),
        ),
        out_specs=P(None, "col", "row"),
        check_vma=False,
    )
```

```python
import jax
import jax.numpy as jnp
from jax import lax
from jax.experimental import pallas as pl
from jax.experimental.pallas import tpu as pltpu
from jax.sharding import PartitionSpec as P

WIN = 128
LANES = 128
EDGE = 2
HIGH = lax.Precision.HIGHEST
ROWS = 8
TAPS = 9


def features_kernel(phase_ref, window_ref, params_ref, hidden_ref, shifted):
    chans = hidden_ref.shape[0]
    tile = window_ref.shape[2]
    width = tile // LANES
    lat = window_ref.shape[1]
    span = WIN * LANES
    total = span + 2 * EDGE * LANES
    lane = lax.broadcasted_iota(jnp.int32, (ROWS, tile), 1) % LANES
    zeros_edge = jnp.zeros((ROWS, EDGE * LANES), jnp.float32)
    for a in range(3):
        shifted[a, :, 0 : EDGE * LANES] = zeros_edge
        shifted[a, :, total - EDGE * LANES : total] = zeros_edge
    for part in range(window_ref.shape[0]):
        cells = window_ref[part].astype(jnp.float32)
        cells = jnp.concatenate([cells, jnp.zeros((ROWS - lat, tile), jnp.float32)], axis=0)
        at = EDGE * LANES + part * tile
        shifted[0, :, at : at + tile] = jnp.where(lane == 0, 0.0, pltpu.roll(cells, 1, 1))
        shifted[1, :, at : at + tile] = cells
        shifted[2, :, at : at + tile] = jnp.where(
            lane == LANES - 1, 0.0, pltpu.roll(cells, tile - 1, 1)
        )

    def tap_views(start, size):
        return [
            shifted[a, :, pl.ds(start + (b - 1) * LANES, size)]
            for a in range(3)
            for b in range(3)
        ]

    depth = TAPS * ROWS
    columns = params_ref[...].T
    w = columns[0:chans, 0:depth]
    w_bf = w.astype(jnp.bfloat16)
    gain = jnp.broadcast_to(columns[0:chans, depth : depth + 1], (chans, LANES))
    shift = jnp.broadcast_to(columns[0:chans, depth + 1 : depth + 2], (chans, LANES))
    count = float(span)
    sums = [jnp.sum(v, axis=1, keepdims=True) for v in tap_views(EDGE * LANES, span)]
    xbar = jnp.concatenate(sums, axis=0) * (1.0 / count)

    def gram_step(step, carry):
        same, cross = carry
        start = pl.multiple_of(EDGE * LANES + step * 2048, LANES)
        cells = jnp.concatenate(
            [
                shifted[a, :, pl.ds(pl.multiple_of(start + (b - 1) * LANES, LANES), 2048)]
                for a in range(3)
                for b in range(3)
            ],
            axis=0,
        )
        centred = cells - xbar
        high = centred.astype(jnp.bfloat16)
        low = (centred - high.astype(jnp.float32)).astype(jnp.bfloat16)
        dims = (((1,), (1,)), ((), ()))
        same = same + lax.dot_general(high, high, dims, preferred_element_type=jnp.float32)
        cross = cross + lax.dot_general(high, low, dims, preferred_element_type=jnp.float32)
        return same, cross

    blank = jnp.zeros((depth, depth), jnp.float32)
    same, cross = lax.fori_loop(0, span // 2048, gram_step, (blank, blank))
    spread = (same + 2.0 * cross) * (1.0 / count)
    chan_mean = jnp.dot(
        w, jnp.broadcast_to(xbar, (depth, LANES)), precision=HIGH, preferred_element_type=jnp.float32
    )
    quad = jnp.dot(w, spread, precision=HIGH, preferred_element_type=jnp.float32) * w
    chan_var = jnp.sum(quad, axis=1, keepdims=True)
    of_row = (lax.broadcasted_iota(jnp.int32, (chans, chans), 0) * 6554) >> 16
    of_col = (lax.broadcasted_iota(jnp.int32, (chans, chans), 1) * 6554) >> 16
    member = (of_row == of_col).astype(jnp.float32)
    mean = jnp.dot(member, chan_mean, precision=HIGH, preferred_element_type=jnp.float32) * 0.1
    off = chan_mean - mean
    var = jnp.dot(member, chan_var + off * off, precision=HIGH, preferred_element_type=jnp.float32) * 0.1
    scale = 0.5 * gain / jnp.sqrt(var + 1e-05)
    base = 0.5 * shift - mean * scale

    phase = phase_ref[0]
    first, last = phase == 0, phase == 3
    scale2 = jnp.concatenate([scale, scale], axis=1)
    base2 = jnp.concatenate([base, base], axis=1)
    pairs = (width + 2) // 2
    for pair in range(pairs):
        start = phase * tile + pair * 2 * LANES
        cells = jnp.concatenate(
            [
                shifted[a, :, pl.ds(pl.multiple_of(start + b * LANES, LANES), 2 * LANES)]
                for a in range(3)
                for b in range(3)
            ],
            axis=0,
        ).astype(jnp.bfloat16)
        feat = jnp.dot(w_bf, cells, preferred_element_type=jnp.float32)
        half = feat * scale2 + base2
        act = half * jnp.tanh(half) + half
        if pair == 0:
            act = jnp.concatenate([jnp.where(first, 0.0, act[:, :LANES]), act[:, LANES:]], axis=1)
        if pair == pairs - 1:
            act = jnp.concatenate([act[:, :LANES], jnp.where(last, 0.0, act[:, LANES:])], axis=1)
        hidden_ref[:, pair * 2 * LANES : (pair + 1) * 2 * LANES] = act.astype(jnp.bfloat16)


def features(phase, window, params, chans):
    width = window.shape[2] // LANES
    return pl.pallas_call(
        features_kernel,
        out_shape=jax.ShapeDtypeStruct((chans, (width + 2) * LANES), jnp.bfloat16),
        in_specs=[pl.BlockSpec(memory_space=pltpu.SMEM)] + [pl.BlockSpec(memory_space=pltpu.VMEM)] * 2,
        out_specs=pl.BlockSpec(memory_space=pltpu.VMEM),
        scratch_shapes=[pltpu.VMEM((3, ROWS, (WIN + 2 * EDGE) * LANES), jnp.float32)],
        compiler_params=pltpu.CompilerParams(vmem_limit_bytes=16 * 2**20),
        name="features",
    )(phase, window, params)


KPAD = 512
COLS = 4
HALF_COLS = 16
BLOCK = 80
VMEM = pl.BlockSpec(memory_space=pltpu.VMEM)
SMEM = pl.BlockSpec(memory_space=pltpu.SMEM)


def split_float(value):
    high = value.astype(jnp.bfloat16).astype(jnp.float32)
    return high, value - high


LOW = pltpu.CompilerParams(vmem_limit_bytes=8 * 2**20)


def prepare_kernel(
    w_conv_ref,
    third_ref,
    latent_ref,
    step_ref,
    one_ref,
    two_ref,
    w_in_ref,
    gain_ref,
    shift_ref,
    shard_ref,
    own_ref,
    params_ref,
    rows,
):
    shard, chans = w_conv_ref.shape[1:]
    half, temb_half = chans // 2, third_ref.shape[1] // 2
    temb = two_ref.shape[1]
    own_ref[...] = latent_ref[...].astype(jnp.bfloat16)
    lat, depth = w_in_ref.shape[1], TAPS * ROWS
    params_ref[...] = jnp.zeros(params_ref.shape, jnp.float32)
    for tap in range(TAPS):
        params_ref[tap * ROWS : tap * ROWS + lat, 0:chans] = w_in_ref[tap].astype(jnp.float32)
    params_ref[depth : depth + 1, 0:chans] = gain_ref[...].reshape(1, chans)
    params_ref[depth + 1 : depth + 2, 0:chans] = shift_ref[...].reshape(1, chans)
    rows[...] = jnp.zeros(rows.shape, jnp.float32)
    wide = rows.shape[1] // 2
    for h in range(2):
        for a in range(3):
            for b in range(3):
                at = h * wide + a * KPAD + b * half
                rows[0:shard, at : at + half] = w_conv_ref[
                    3 * a + b, :, h * half : (h + 1) * half
                ].astype(jnp.float32)
        at = h * wide + 3 * KPAD
        rows[0:shard, at : at + temb_half] = third_ref[:, h * temb_half : (h + 1) * temb_half].astype(
            jnp.float32
        )
    lane = lax.broadcasted_iota(jnp.int32, (8, chans), 1)
    k = jnp.where(lane < half, lane, lane - half).astype(jnp.float32)
    freq = jnp.exp(-jnp.log(jnp.float32(10000.0)) * k / jnp.float32(half))
    angle = step_ref[...].astype(jnp.float32) * freq
    emb = jnp.where(lane < half, jnp.cos(angle), jnp.sin(angle))
    first = lax.dot_general(
        emb,
        one_ref[...].astype(jnp.float32),
        (((1,), (1,)), ((), ())),
        precision=HIGH,
        preferred_element_type=jnp.float32,
    )
    first = (first / (1.0 + jnp.exp(-first))).astype(jnp.bfloat16)
    second = jnp.dot(first, two_ref[...], preferred_element_type=jnp.float32)
    high, low = split_float(second[0:1])
    rows[shard : shard + 1, 0:temb] = high
    rows[shard + 1 : shard + 2, 0:temb] = low
    shard_ref[...] = rows[...].astype(jnp.bfloat16)


def prepare(w_conv, third, latent, step, w_one, w_two, w_in, gain, shift):
    wide = 6 * KPAD + third.shape[1]
    inputs = (w_conv, third, latent, step, w_one, w_two, w_in, gain, shift)
    return pl.pallas_call(
        prepare_kernel,
        out_shape=(
            jax.ShapeDtypeStruct((16, wide), jnp.bfloat16),
            jax.ShapeDtypeStruct(latent.shape, jnp.bfloat16),
            jax.ShapeDtypeStruct((LANES, 3 * LANES), jnp.float32),
        ),
        in_specs=[VMEM] * len(inputs),
        out_specs=(VMEM,) * 3,
        scratch_shapes=[pltpu.VMEM((16, wide), jnp.float32)],
        name="prepare",
    )(*inputs)


def theirs_kernel(place_ref, *rest):
    parts, out_ref = rest[:4], rest[4]
    core, z_lo = place_ref[0], place_ref[1]
    wide = out_ref.shape[2]
    for k in range(4):
        out_ref[(z_lo + k) % 4] = parts[k][:, pl.ds(pl.multiple_of((1 - core) * wide, LANES), wide)]


def for_other_core(place, parts):
    rows, wide = parts[0].shape
    return pl.pallas_call(
        theirs_kernel,
        out_shape=jax.ShapeDtypeStruct((4, rows, wide // 2), parts[0].dtype),
        in_specs=[SMEM] + [VMEM] * 4,
        out_specs=VMEM,
        compiler_params=LOW,
        name="for_other_core",
    )(place, *parts)


def block_kernel(place_ref, got_ref, *rest):
    parts, out_ref, held, rows = rest[:4], rest[4], rest[5], rest[6]
    core, z_lo = place_ref[0], place_ref[1]
    wide = out_ref.shape[1]
    shard = BLOCK // 8
    temb = 2 * (wide - 3 * KPAD)
    total = jnp.zeros((1, temb), jnp.float32)
    for k in range(4):
        part = parts[k][:, pl.ds(pl.multiple_of(core * wide, LANES), wide)]
        held[(z_lo + k) % 4] = part.astype(jnp.float32)
        two = parts[k][:, 0:temb].astype(jnp.float32)
        total = total + two[shard : shard + 1] + two[shard + 1 : shard + 2]
    for k in range(4):
        mine, got = held[k], got_ref[k].astype(jnp.float32)
        at = 2 * shard * k
        rows[at : at + 16, :] = jnp.where(core == 0, mine, got)
        rows[at + shard : at + shard + 16, :] = jnp.where(core == 0, got, mine)
    rows[BLOCK : BLOCK + 8, :] = jnp.zeros((8, wide), jnp.float32)
    high, low = split_float(total)
    rows[BLOCK : BLOCK + 1, :temb] = high
    rows[BLOCK + 1 : BLOCK + 2, :temb] = low
    out_ref[...] = rows[0 : BLOCK + 8, :].astype(jnp.bfloat16)


def make_block(place, got, parts):
    wide = got.shape[2]
    return pl.pallas_call(
        block_kernel,
        out_shape=jax.ShapeDtypeStruct((BLOCK + 8, wide), jnp.bfloat16),
        in_specs=[SMEM] + [VMEM] * 5,
        out_specs=VMEM,
        scratch_shapes=[
            pltpu.VMEM((4, 16, wide), jnp.float32),
            pltpu.VMEM((BLOCK + 16, wide), jnp.float32),
        ],
        compiler_params=LOW,
        name="make_block",
    )(place, got, *parts)


def pick(rows, cols, offset, down):
    source = lax.broadcasted_iota(jnp.int32, (rows, cols), 1 if down else 0)
    target = lax.broadcasted_iota(jnp.int32, (rows, cols), 0 if down else 1)
    return jnp.where(source == target + offset, 1.0, 0.0).astype(jnp.bfloat16)


def strip_kernel(offset_ref, own_ref, beside_ref, out_ref):
    width = own_ref.shape[1]
    chosen = pick(width, 2 * width, offset_ref[...], True)
    for c in range(own_ref.shape[0]):
        both = jnp.concatenate([own_ref[c], beside_ref[c]], axis=0)
        out_ref[c] = jnp.dot(chosen, both, preferred_element_type=jnp.float32).astype(jnp.bfloat16)


def moved_kernel(offset_ref, strip_ref, below_ref, out_ref):
    height = strip_ref.shape[2]
    chosen = pick(2 * height, height, offset_ref[...], False)
    for c in range(strip_ref.shape[0]):
        both = jnp.concatenate([strip_ref[c], below_ref[c]], axis=1)
        out_ref[c] = jnp.dot(both, chosen, preferred_element_type=jnp.float32).astype(jnp.bfloat16)


def shift(kernel, offset, first, second, name):
    return pl.pallas_call(
        kernel,
        out_shape=jax.ShapeDtypeStruct(first.shape, first.dtype),
        in_specs=[VMEM] * 3,
        out_specs=VMEM,
        compiler_params=LOW,
        name=name,
    )(offset.reshape(1, 1), first, second)


def conv_kernel(place_ref, hidden_ref, *rest):
    refs, (out_ref, prod_a, prod_b, wide, staged, sems) = rest[:8], rest[8:]
    prods = (prod_a, prod_b)
    core, xpos = place_ref[0], place_ref[2]
    chans = hidden_ref.shape[0]
    half = chans // 2
    own = pl.multiple_of(core * half, 16)
    other = pl.multiple_of((1 - core) * half, 16)
    n = COLS * LANES
    temb_half = refs[0].shape[1] - 3 * KPAD
    lane = lax.broadcasted_iota(jnp.int32, (BLOCK, n), 1) % LANES

    def block(side, k, first, last):
        return refs[4 * side + k][0:BLOCK, first:last]

    second = jnp.zeros((1, 2 * temb_half), jnp.float32)
    for ref in refs:
        two = ref[BLOCK : BLOCK + 8, 0 : 2 * temb_half].astype(jnp.float32)
        second = second + two[0:1] + two[1:2]
    s_two = second / (1.0 + jnp.exp(-second))
    s_two = s_two.astype(jnp.bfloat16).astype(jnp.float32)
    s_low, s_high = s_two[:, :temb_half], s_two[:, temb_half:]
    s_sides = (jnp.where(core == 0, s_low, s_high), jnp.where(core == 0, s_high, s_low))
    tvecs = []
    for k in range(4):
        terms = [
            block(side, k, 3 * KPAD, 3 * KPAD + temb_half).astype(jnp.float32) * s_sides[side]
            for side in range(2)
        ]
        tvecs.append(jnp.sum(terms[0] + terms[1], axis=1, keepdims=True))

    def multiply(col, prod):
        right = []
        for rows in (own, other):
            for b in range(3):
                at = (col + b) * LANES
                right.append(hidden_ref[pl.ds(rows, half), at : at + n])
            right.append(right[-1][0 : KPAD - 3 * half])
        right = jnp.concatenate(right, axis=0)
        left = jnp.concatenate(
            [
                jnp.concatenate([block(side, k, a * KPAD, (a + 1) * KPAD) for side in range(2)], axis=1)
                for k in range(4)
                for a in range(3)
            ],
            axis=0,
        )
        prod[...] = jnp.dot(left, right, preferred_element_type=jnp.float32)

    def finish(local, prod):
        for k in range(4):
            at = 3 * k * BLOCK
            low = prod[at : at + BLOCK, :]
            mid = prod[at + BLOCK : at + 2 * BLOCK, :]
            high = prod[at + 2 * BLOCK : at + 3 * BLOCK, :]
            done = (
                mid
                + jnp.where(lane == 0, 0.0, pltpu.roll(low, 1, 1))
                + jnp.where(lane == LANES - 1, 0.0, pltpu.roll(high, n - 1, 1))
                + tvecs[k]
            )
            chan = (xpos + (0, 1, 3, 2)[k]) % 4 * BLOCK
            for j in range(COLS):
                first = chan * HALF_COLS + local + j
                wide[pl.ds(first, BLOCK, stride=HALF_COLS), :] = done[:, j * LANES : (j + 1) * LANES]

    width = out_ref.shape[1]
    tiles, per = width // COLS, HALF_COLS // COLS
    copies = []
    for t in range(tiles + 1):
        if t < tiles:
            multiply(t * COLS, prods[t % 2])
        if t > 0:
            finish((t - 1) % per * COLS, prods[(t - 1) % 2])
            if t % per == 0:
                h = t // per - 1
                staged[h] = wide[...].reshape(chans, HALF_COLS, LANES).astype(jnp.bfloat16)
                copy = pltpu.make_async_copy(
                    staged.at[h], out_ref.at[:, pl.ds(h * HALF_COLS, HALF_COLS), :], sems.at[h]
                )
                copy.start()
                copies.append(copy)
    for copy in copies:
        copy.wait()


def conv(place, hidden, pieces):
    chans, padded = hidden.shape
    width = padded // LANES - 2
    halves = width // HALF_COLS
    return pl.pallas_call(
        conv_kernel,
        out_shape=jax.ShapeDtypeStruct((chans, width, LANES), jnp.bfloat16),
        in_specs=[SMEM] + [VMEM] * (1 + len(pieces)),
        out_specs=pl.BlockSpec(memory_space=pl.ANY),
        scratch_shapes=[
            pltpu.VMEM((3 * chans, COLS * LANES), jnp.float32),
            pltpu.VMEM((3 * chans, COLS * LANES), jnp.float32),
            pltpu.VMEM((chans * HALF_COLS, LANES), jnp.float32),
            pltpu.VMEM((halves, chans, HALF_COLS, LANES), jnp.bfloat16),
            pltpu.SemaphoreType.DMA((halves,)),
        ],
        compiler_params=pltpu.CompilerParams(vmem_limit_bytes=20 * 2**20),
        name="convolve",
    )(place, hidden, *pieces)


def pairs_of(move):
    pairs = []
    for row in range(8):
        for col in range(32):
            y, z_hi, x, z_lo, core = row // 2, row % 2, col // 8, col // 2 % 4, col % 2
            z = z_hi * 4 + z_lo
            y, z, x, core = move(y, z, x, core)
            y, z, x = y % 4, z % 8, x % 4
            pairs.append((row * 32 + col, (y * 2 + z // 4) * 32 + x * 8 + z % 4 * 2 + core))
    return pairs


def send(value, move):
    return lax.ppermute(value, ("row", "col"), pairs_of(move))


def fetch_grid(value, rows, cols):
    pairs = [
        ((r + rows) % 8 * 32 + (c + cols) % 32, r * 32 + c) for r in range(8) for c in range(32)
    ]
    return lax.ppermute(value, ("row", "col"), pairs)


def swap_core(value):
    return send(value, lambda y, z, x, core: (y, z, x, 1 - core))


def from_z(value, steps):
    return send(value, lambda y, z, x, core: (y, z - steps, x, core))


def from_x(value, steps):
    return send(value, lambda y, z, x, core: (y, z, x - steps, core))


WINDOW_GROUPS = [[r * 32 + (4 * p + 2 + k) % 32 for k in range(4)] for r in range(8) for p in range(8)]


def body(
    latent,
    row_offset,
    col_offset,
    timestep,
    w_in,
    norm_gain,
    norm_shift,
    w_conv,
    w_time1,
    w_time2,
    w_time3,
):
    chans, lat = w_in.shape[1:]
    width, height = latent.shape[1:]
    col = lax.axis_index("col")
    core, z_lo, x = col % 2, col // 2 % 4, col // 8
    phase = (col + 30) % 4

    shard, own, params = prepare(
        w_conv,
        w_time3.T,
        latent,
        timestep.reshape(1, 1),
        w_time1.T,
        w_time2,
        w_in.transpose(0, 2, 1),
        norm_gain,
        norm_shift,
    )
    beside = fetch_grid(own, 0, 1)
    near = [shard, from_z(shard, 1), from_z(shard, 2), from_z(shard, -1)]
    strip = shift(strip_kernel, col_offset, own, beside, "strip")
    below = fetch_grid(strip, 1, 0)
    place = jnp.stack([core, z_lo, x])
    near, below = lax.optimization_barrier((near, below))
    got = swap_core(for_other_core(place, near))
    block = make_block(place, got, near)
    after, before, across = from_x(block, 1), from_x(block, -1), from_x(block, 2)

    moved = shift(moved_kernel, row_offset, strip, below, "moved")
    window = lax.all_gather(
        moved.reshape(lat, width * height), ("row", "col"), axis_index_groups=WINDOW_GROUPS, axis=0
    )
    hidden = features(phase[None], window, params, chans)
    far = lax.optimization_barrier((after, before, across, hidden))
    after, before, across, hidden = far
    pieces = [block, after, before, across]
    pieces = pieces + [swap_core(v) for v in pieces]
    return conv(place, hidden, pieces)


def solution(mesh):
    return jax.shard_map(
        body,
        mesh=mesh,
        in_specs=(
            P(None, "col", "row"),
            P(),
            P(),
            P(),
            P(),
            P(),
            P(),
            P(None, "col", None),
            P(None, "col"),
            P("col", None),
            P(None, "col"),
        ),
        out_specs=P(None, "col", "row"),
        check_vma=False,
    )
```

```python
import jax
import jax.numpy as jnp
from jax import lax
from jax.experimental import pallas as pl
from jax.experimental.pallas import tpu as pltpu
from jax.sharding import PartitionSpec as P

WIN = 128
LANES = 128
EDGE = 2
HIGH = lax.Precision.HIGHEST
ROWS = 8
DEPTH = 6 * ROWS


def features_kernel(window_ref, params_ref, hidden_ref, shifted):
    chans = hidden_ref.shape[0]
    tile = window_ref.shape[2]
    width = tile // LANES
    lat = window_ref.shape[1]
    span = WIN * LANES
    total = span + 2 * EDGE * LANES
    lane = lax.broadcasted_iota(jnp.int32, (ROWS, tile), 1) % LANES
    zeros_edge = jnp.zeros((ROWS, EDGE * LANES), jnp.float32)
    for a in range(3):
        shifted[a, :, 0 : EDGE * LANES] = zeros_edge
        shifted[a, :, total - EDGE * LANES : total] = zeros_edge
        shifted[a, :, total - (EDGE + 1) * LANES : total - EDGE * LANES] = zeros_edge[:, :LANES]
    for part in range(window_ref.shape[0]):
        cells = window_ref[part].astype(jnp.float32)
        cells = jnp.concatenate([cells, cells], axis=0)
        at = EDGE * LANES + part * tile
        views = (
            jnp.where(lane == 0, 0.0, pltpu.roll(cells, 1, 1)),
            cells,
            jnp.where(lane == LANES - 1, 0.0, pltpu.roll(cells, tile - 1, 1)),
        )
        for a, view in enumerate(views):
            shifted[a, 0:lat, at : at + tile] = view[0:lat]
            shifted[a, lat : 2 * lat, at - LANES : at + tile - LANES] = view[lat : 2 * lat]

    def patches(start, size):
        return jnp.concatenate(
            [shifted[a, :, pl.ds(start + 2 * b * LANES, size)] for a in range(3) for b in range(2)],
            axis=0,
        )

    depth = DEPTH
    columns = params_ref[...].T
    w = columns[0:chans, 0:depth]
    w_bf = w.astype(jnp.bfloat16)
    gain = jnp.broadcast_to(columns[0:chans, depth : depth + 1], (chans, LANES))
    shift = jnp.broadcast_to(columns[0:chans, depth + 1 : depth + 2], (chans, LANES))
    count = float(span)
    first_cell = (EDGE - 1) * LANES
    xbar = jnp.sum(patches(first_cell, span), axis=1, keepdims=True) * (1.0 / count)
    same = jnp.zeros((depth, depth), jnp.float32)
    cross = same
    chunk = 2048
    dims = (((1,), (1,)), ((), ()))
    for step in range(span // chunk):
        centred = patches(first_cell + step * chunk, chunk) - xbar
        high = centred.astype(jnp.bfloat16)
        low = (centred - high.astype(jnp.float32)).astype(jnp.bfloat16)
        same = same + lax.dot_general(high, high, dims, preferred_element_type=jnp.float32)
        cross = cross + lax.dot_general(high, low, dims, preferred_element_type=jnp.float32)
    spread = (same + 2.0 * cross) * (1.0 / count)
    chan_mean = jnp.dot(
        w, jnp.broadcast_to(xbar, (depth, LANES)), precision=HIGH, preferred_element_type=jnp.float32
    )
    quad = jnp.dot(w, spread, precision=HIGH, preferred_element_type=jnp.float32) * w
    chan_var = jnp.sum(quad, axis=1, keepdims=True)
    of_row = (lax.broadcasted_iota(jnp.int32, (chans, chans), 0) * 6554) >> 16
    of_col = (lax.broadcasted_iota(jnp.int32, (chans, chans), 1) * 6554) >> 16
    member = (of_row == of_col).astype(jnp.float32)
    mean = jnp.dot(member, chan_mean, precision=HIGH, preferred_element_type=jnp.float32) * 0.1
    off = chan_mean - mean
    var = jnp.dot(member, chan_var + off * off, precision=HIGH, preferred_element_type=jnp.float32) * 0.1
    scale = 0.5 * gain / jnp.sqrt(var + 1e-05)
    base = 0.5 * shift - mean * scale

    phase = lax.rem(lax.axis_index("col") + 30, 4)
    first, last = phase == 0, phase == 3
    scale2 = jnp.concatenate([scale, scale], axis=1)
    base2 = jnp.concatenate([base, base], axis=1)
    pairs = (width + 2) // 2
    for pair in range(pairs):
        start = phase * tile + pair * 2 * LANES
        cells = jnp.concatenate(
            [
                shifted[a, :, pl.ds(pl.multiple_of(start + 2 * b * LANES, LANES), 2 * LANES)]
                for a in range(3)
                for b in range(2)
            ],
            axis=0,
        ).astype(jnp.bfloat16)
        feat = jnp.dot(w_bf, cells, preferred_element_type=jnp.float32)
        half = feat * scale2 + base2
        act = half * jnp.tanh(half) + half
        if pair == 0:
            act = jnp.concatenate([jnp.where(first, 0.0, act[:, :LANES]), act[:, LANES:]], axis=1)
        if pair == pairs - 1:
            act = jnp.concatenate([act[:, :LANES], jnp.where(last, 0.0, act[:, LANES:])], axis=1)
        hidden_ref[:, pair * 2 * LANES : (pair + 1) * 2 * LANES] = act.astype(jnp.bfloat16)


def features(window, params, chans):
    width = window.shape[2] // LANES
    return pl.pallas_call(
        features_kernel,
        out_shape=jax.ShapeDtypeStruct((chans, (width + 2) * LANES), jnp.bfloat16),
        in_specs=[pl.BlockSpec(memory_space=pltpu.VMEM)] * 2,
        out_specs=pl.BlockSpec(memory_space=pltpu.VMEM),
        scratch_shapes=[pltpu.VMEM((3, ROWS, (WIN + 2 * EDGE) * LANES), jnp.float32)],
        compiler_params=pltpu.CompilerParams(vmem_limit_bytes=16 * 2**20),
        name="features",
    )(in_vmem(window), in_vmem(params))


KPAD = 512
COLS = 4
HALF_COLS = 16
BLOCK = 80
VMEM = pl.BlockSpec(memory_space=pltpu.VMEM)
SMEM = pl.BlockSpec(memory_space=pltpu.SMEM)


def position():
    col = lax.axis_index("col")
    return lax.rem(col, 2), lax.rem(lax.div(col, 2), 4), lax.div(col, 8)


def in_vmem(value):
    return pltpu.with_memory_space_constraint(value, pltpu.VMEM)


def split_float(value):
    high = value.astype(jnp.bfloat16).astype(jnp.float32)
    return high, value - high


LOW = pltpu.CompilerParams(vmem_limit_bytes=8 * 2**20)


def prepare_kernel(*rest):
    w_conv_ref, third_ref, latent_ref, one_ref, two_ref, w_in_ref = rest[15:21]
    gain_ref, shift_ref, steps_ref = rest[21:24]
    rows, sems = rest[24:]
    copies = [pltpu.make_async_copy(rest[i], rest[15 + i], sems.at[i]) for i in range(9)]
    for copy in copies:
        copy.start()
    mine_ref, theirs_ref, own_ref, part_ref, params_ref, offsets_ref = rest[9:15]
    core, _, _ = position()
    shard, chans = w_conv_ref.shape[1:]
    half, temb_half = chans // 2, third_ref.shape[1] // 2
    rows[...] = jnp.zeros(rows.shape, jnp.float32)
    params_ref[...] = jnp.zeros(params_ref.shape, jnp.float32)
    lane = lax.broadcasted_iota(jnp.int32, (8, chans), 1)
    k = jnp.where(lane < half, lane, lane - half).astype(jnp.float32)
    freq = jnp.exp(-jnp.log(jnp.float32(10000.0)) * k / jnp.float32(half))
    for copy in copies:
        copy.wait()
    offsets_ref[...] = steps_ref[...]
    own_ref[...] = latent_ref[...].astype(jnp.bfloat16)
    for h in range(2):
        for a in range(3):
            for b in range(3):
                at = a * KPAD + b * half
                rows[h, 0:shard, at : at + half] = w_conv_ref[
                    3 * a + b, :, h * half : (h + 1) * half
                ].astype(jnp.float32)
        rows[h, 0:shard, 3 * KPAD :] = third_ref[:, h * temb_half : (h + 1) * temb_half].astype(
            jnp.float32
        )
    mine_ref[...] = rows[core].astype(jnp.bfloat16)
    theirs_ref[...] = rows[1 - core].astype(jnp.bfloat16)
    lat, depth = w_in_ref.shape[1], DEPTH
    for tap in range(w_in_ref.shape[0]):
        at = tap // 3 * 2 * ROWS + tap % 3 * lat
        params_ref[at : at + lat, 0:chans] = w_in_ref[tap].astype(jnp.float32)
    params_ref[depth : depth + 1, 0:chans] = gain_ref[...].reshape(1, chans)
    params_ref[depth + 1 : depth + 2, 0:chans] = shift_ref[...].reshape(1, chans)
    angle = steps_ref[2:3, 0:1].astype(jnp.float32) * freq
    emb = jnp.where(lane < half, jnp.cos(angle), jnp.sin(angle))
    first = lax.dot_general(
        emb,
        one_ref[...].astype(jnp.float32),
        (((1,), (1,)), ((), ())),
        precision=HIGH,
        preferred_element_type=jnp.float32,
    )
    first = (first / (1.0 + jnp.exp(-first))).astype(jnp.bfloat16)
    second = jnp.dot(first, two_ref[...], preferred_element_type=jnp.float32)
    high, low = split_float(second)
    row = lax.broadcasted_iota(jnp.int32, second.shape, 0)
    part_ref[...] = jnp.where(row == 0, high, jnp.where(row == 1, low, 0.0))


def prepare(w_conv, third, latent, w_one, w_two, w_in, gain, shift, steps):
    wide = 3 * KPAD + third.shape[1] // 2
    inputs = (w_conv, third, latent, w_one, w_two, w_in, gain, shift, steps)
    inputs = [pltpu.with_memory_space_constraint(v, pltpu.HBM) for v in inputs]
    return pl.pallas_call(
        prepare_kernel,
        out_shape=(
            jax.ShapeDtypeStruct((16, wide), jnp.bfloat16),
            jax.ShapeDtypeStruct((16, wide), jnp.bfloat16),
            jax.ShapeDtypeStruct(latent.shape, jnp.bfloat16),
            jax.ShapeDtypeStruct((8, w_two.shape[1]), jnp.float32),
            jax.ShapeDtypeStruct((LANES, 3 * LANES), jnp.float32),
            jax.ShapeDtypeStruct(steps.shape, steps.dtype),
        ),
        in_specs=[pl.BlockSpec(memory_space=pltpu.HBM)] * len(inputs),
        out_specs=(VMEM,) * 6,
        scratch_shapes=[pltpu.VMEM(v.shape, v.dtype) for v in inputs]
        + [pltpu.VMEM((2, 16, wide), jnp.float32), pltpu.SemaphoreType.DMA((len(inputs),))],
        compiler_params=LOW,
        name="prepare",
    )(*inputs)


def pair_kernel(mine_ref, got_ref, time_ref, out_ref, rows):
    core, _, _ = position()
    shard = 10
    temb = time_ref.shape[1]
    mine = mine_ref[...].astype(jnp.float32)
    got = got_ref[...].astype(jnp.float32)
    rows[0:16, :] = jnp.where(core == 0, mine, got)
    rows[shard : shard + 16, :] = jnp.where(core == 0, got, mine)
    rows[2 * shard : 2 * shard + 8, 0:temb] = time_ref[...]
    out_ref[...] = rows[0:24, :].astype(jnp.bfloat16)


def pair_up(mine, got, part):
    wide = mine.shape[1]
    return pl.pallas_call(
        pair_kernel,
        out_shape=jax.ShapeDtypeStruct((24, wide), jnp.bfloat16),
        in_specs=[VMEM] * 3,
        out_specs=VMEM,
        scratch_shapes=[pltpu.VMEM((32, wide), jnp.float32)],
        compiler_params=LOW,
        name="pair_up",
    )(in_vmem(mine), in_vmem(got), in_vmem(part))


def block_kernel(*rest):
    parts, out_ref, held, rows = rest[:4], rest[4], rest[5], rest[6]
    _, z_lo, _ = position()
    temb = 1280
    total = jnp.zeros((1, temb), jnp.float32)
    for k in range(4):
        part = parts[k][...].astype(jnp.float32)
        total = total + part[20:21, :temb] + part[21:22, :temb]
        held[(z_lo + k) % 4] = part
    for k in range(4):
        rows[20 * k : 20 * k + 24, :] = held[k]
    rows[80:88, :] = jnp.zeros((8, rows.shape[1]), jnp.float32)
    high, low = split_float(total)
    rows[80:81, :temb] = high
    rows[81:82, :temb] = low
    out_ref[...] = rows[...].astype(jnp.bfloat16)


def make_block(parts):
    wide = parts[0].shape[1]
    return pl.pallas_call(
        block_kernel,
        out_shape=jax.ShapeDtypeStruct((88, wide), jnp.bfloat16),
        in_specs=[VMEM] * 4,
        out_specs=VMEM,
        scratch_shapes=[pltpu.VMEM((4, 24, wide), jnp.float32), pltpu.VMEM((88, wide), jnp.float32)],
        compiler_params=LOW,
        name="make_block",
    )(*[in_vmem(v) for v in parts])


def pick(rows, cols, offset, down):
    source = lax.broadcasted_iota(jnp.int32, (rows, cols), 1 if down else 0)
    target = lax.broadcasted_iota(jnp.int32, (rows, cols), 0 if down else 1)
    return jnp.where(source == target + offset, 1.0, 0.0).astype(jnp.bfloat16)


def strip_kernel(offset_ref, own_ref, beside_ref, out_ref):
    width = own_ref.shape[1]
    chosen = pick(width, 2 * width, offset_ref[1:2, 0:1], True)
    for c in range(own_ref.shape[0]):
        both = jnp.concatenate([own_ref[c], beside_ref[c]], axis=0)
        out_ref[c] = jnp.dot(chosen, both, preferred_element_type=jnp.float32).astype(jnp.bfloat16)


def moved_kernel(offset_ref, strip_ref, below_ref, out_ref, stacked, flat):
    lat, width, height = strip_ref.shape
    chosen = pick(2 * height, height, offset_ref[0:1, 0:1], False)
    for c in range(lat):
        both = jnp.concatenate([strip_ref[c], below_ref[c]], axis=1)
        stacked[c * width : (c + 1) * width, :] = jnp.dot(
            both, chosen, preferred_element_type=jnp.float32
        )
    for j in range(width):
        flat[0:lat, j * height : (j + 1) * height] = stacked[pl.ds(j, lat, stride=width), :]
    out_ref[0] = flat[0:lat, :].astype(jnp.bfloat16)


def shift_columns(offset, own, beside):
    return pl.pallas_call(
        strip_kernel,
        out_shape=jax.ShapeDtypeStruct(own.shape, own.dtype),
        in_specs=[VMEM] * 3,
        out_specs=VMEM,
        compiler_params=LOW,
        name="strip",
    )(in_vmem(offset), in_vmem(own), in_vmem(beside))


def shift_rows(offset, strip, below):
    lat, width, height = strip.shape
    return pl.pallas_call(
        moved_kernel,
        out_shape=jax.ShapeDtypeStruct((1, lat, width * height), strip.dtype),
        in_specs=[VMEM] * 3,
        out_specs=VMEM,
        scratch_shapes=[
            pltpu.VMEM((lat * width, height), jnp.float32),
            pltpu.VMEM((ROWS, width * height), jnp.float32),
        ],
        compiler_params=LOW,
        name="moved",
    )(in_vmem(offset), in_vmem(strip), in_vmem(below))


def conv_kernel(hidden_ref, *rest):
    refs, (out_ref, prod_a, prod_b, wide, staged, sems) = rest[:8], rest[8:]
    prods = (prod_a, prod_b)
    core, _, xpos = position()
    chans = hidden_ref.shape[0]
    half = chans // 2
    own = pl.multiple_of(core * half, 16)
    other = pl.multiple_of((1 - core) * half, 16)
    n = COLS * LANES
    temb_half = refs[0].shape[1] - 3 * KPAD
    lane = lax.broadcasted_iota(jnp.int32, (BLOCK, n), 1) % LANES

    def block(side, k, first, last):
        return refs[4 * side + k][0:BLOCK, first:last]

    second = jnp.zeros((1, 2 * temb_half), jnp.float32)
    for ref in refs:
        two = ref[BLOCK : BLOCK + 8, 0 : 2 * temb_half].astype(jnp.float32)
        second = second + two[0:1] + two[1:2]
    s_two = second / (1.0 + jnp.exp(-second))
    s_two = s_two.astype(jnp.bfloat16).astype(jnp.float32)
    s_low, s_high = s_two[:, :temb_half], s_two[:, temb_half:]
    s_sides = (jnp.where(core == 0, s_low, s_high), jnp.where(core == 0, s_high, s_low))
    tvecs = []
    for k in range(4):
        terms = [
            block(side, k, 3 * KPAD, 3 * KPAD + temb_half).astype(jnp.float32) * s_sides[side]
            for side in range(2)
        ]
        tvecs.append(jnp.sum(terms[0] + terms[1], axis=1, keepdims=True))

    def multiply(col, prod):
        right = []
        for rows in (own, other):
            for b in range(3):
                at = (col + b) * LANES
                right.append(hidden_ref[pl.ds(rows, half), at : at + n])
            right.append(right[-1][0 : KPAD - 3 * half])
        right = jnp.concatenate(right, axis=0)
        left = jnp.concatenate(
            [
                jnp.concatenate([block(side, k, a * KPAD, (a + 1) * KPAD) for side in range(2)], axis=1)
                for k in range(4)
                for a in range(3)
            ],
            axis=0,
        )
        prod[...] = jnp.dot(left, right, preferred_element_type=jnp.float32)

    def finish(local, prod):
        for k in range(4):
            at = 3 * k * BLOCK
            low = prod[at : at + BLOCK, :]
            mid = prod[at + BLOCK : at + 2 * BLOCK, :]
            high = prod[at + 2 * BLOCK : at + 3 * BLOCK, :]
            done = (
                mid
                + jnp.where(lane == 0, 0.0, pltpu.roll(low, 1, 1))
                + jnp.where(lane == LANES - 1, 0.0, pltpu.roll(high, n - 1, 1))
                + tvecs[k]
            )
            chan = (xpos + (0, 1, 3, 2)[k]) % 4 * BLOCK
            for j in range(COLS):
                first = chan * HALF_COLS + local + j
                wide[pl.ds(first, BLOCK, stride=HALF_COLS), :] = done[:, j * LANES : (j + 1) * LANES]

    width = out_ref.shape[1]
    tiles, per = width // COLS, HALF_COLS // COLS
    copies = []
    for t in range(tiles + 1):
        if t < tiles:
            multiply(t * COLS, prods[t % 2])
        if t > 0:
            finish((t - 1) % per * COLS, prods[(t - 1) % 2])
            if t % per == 0:
                h = t // per - 1
                parts = 1 if t < tiles else 4
                size = chans // parts
                for part in range(parts):
                    at = part * size
                    cells = wide[at * HALF_COLS : (at + size) * HALF_COLS, :]
                    staged[h, at : at + size] = cells.reshape(size, HALF_COLS, LANES).astype(jnp.bfloat16)
                    copy = pltpu.make_async_copy(
                        staged.at[h, pl.ds(at, size)],
                        out_ref.at[pl.ds(at, size), pl.ds(h * HALF_COLS, HALF_COLS), :],
                        sems.at[len(copies)],
                    )
                    copy.start()
                    copies.append(copy)
    for copy in copies:
        copy.wait()


def conv(hidden, pieces):
    chans, padded = hidden.shape
    width = padded // LANES - 2
    halves = width // HALF_COLS
    return pl.pallas_call(
        conv_kernel,
        out_shape=jax.ShapeDtypeStruct((chans, width, LANES), jnp.bfloat16),
        in_specs=[VMEM] * (1 + len(pieces)),
        out_specs=pl.BlockSpec(memory_space=pl.ANY),
        scratch_shapes=[
            pltpu.VMEM((3 * chans, COLS * LANES), jnp.float32),
            pltpu.VMEM((3 * chans, COLS * LANES), jnp.float32),
            pltpu.VMEM((chans * HALF_COLS, LANES), jnp.float32),
            pltpu.VMEM((halves, chans, HALF_COLS, LANES), jnp.bfloat16),
            pltpu.SemaphoreType.DMA((halves + 3,)),
        ],
        compiler_params=pltpu.CompilerParams(vmem_limit_bytes=20 * 2**20),
        name="convolve",
    )(in_vmem(hidden), *[in_vmem(v) for v in pieces])


def pairs_of(move):
    pairs = []
    for row in range(8):
        for col in range(32):
            y, z_hi, x, z_lo, core = row // 2, row % 2, col // 8, col // 2 % 4, col % 2
            z = z_hi * 4 + z_lo
            y, z, x, core = move(y, z, x, core)
            y, z, x = y % 4, z % 8, x % 4
            pairs.append((row * 32 + col, (y * 2 + z // 4) * 32 + x * 8 + z % 4 * 2 + core))
    return pairs


def send(value, move):
    return lax.ppermute(value, ("row", "col"), pairs_of(move))


def fetch_grid(value, rows, cols):
    pairs = [
        ((r + rows) % 8 * 32 + (c + cols) % 32, r * 32 + c) for r in range(8) for c in range(32)
    ]
    return lax.ppermute(value, ("row", "col"), pairs)


def swap_core(value):
    return send(value, lambda y, z, x, core: (y, z, x, 1 - core))


def from_z(value, steps):
    return send(value, lambda y, z, x, core: (y, z - steps, x, core))


def from_x(value, steps):
    return send(value, lambda y, z, x, core: (y, z, x - steps, core))


WINDOW_GROUPS = [[r * 32 + (4 * p + 2 + k) % 32 for k in range(4)] for r in range(8) for p in range(8)]


def body(
    latent,
    row_offset,
    col_offset,
    timestep,
    w_in,
    norm_gain,
    norm_shift,
    w_conv,
    w_time1,
    w_time2,
    w_time3,
):
    chans = w_in.shape[1]
    row = lax.broadcasted_iota(jnp.int32, (8, LANES), 0)
    steps = jnp.where(row == 0, row_offset[:, None], jnp.where(row == 1, col_offset[:, None], timestep[:, None]))
    mine, theirs, own, part, params, offsets = prepare(
        w_conv,
        w_time3.T,
        latent,
        w_time1.T,
        w_time2,
        w_in.transpose(0, 2, 1),
        norm_gain,
        norm_shift,
        steps,
    )
    beside = fetch_grid(own, 0, 1)
    got = swap_core(theirs)
    got, beside = lax.optimization_barrier((got, beside))
    zrow = pair_up(mine, got, part)
    near = [zrow, from_z(zrow, 1), from_z(zrow, 2), from_z(zrow, -1)]
    strip = shift_columns(offsets, own, beside)
    below = fetch_grid(strip, 1, 0)
    near, below = lax.optimization_barrier((near, below))
    block = make_block(near)
    after, before, across = from_x(block, 1), from_x(block, -1), from_x(block, 2)

    moved = shift_rows(offsets, strip, below)
    window = lax.all_gather(
        moved, ("row", "col"), axis_index_groups=WINDOW_GROUPS, axis=0, tiled=True
    )
    hidden = features(window, params, chans)
    far = lax.optimization_barrier((after, before, across, hidden))
    after, before, across, hidden = far
    pieces = [block, after, before, across]
    pieces = pieces + [swap_core(v) for v in pieces]
    return conv(hidden, pieces)


def solution(mesh):
    return jax.shard_map(
        body,
        mesh=mesh,
        in_specs=(
            P(None, "col", "row"),
            P(),
            P(),
            P(),
            P(),
            P(),
            P(),
            P(None, "col", None),
            P(None, "col"),
            P("col", None),
            P(None, "col"),
        ),
        out_specs=P(None, "col", "row"),
        check_vma=False,
    )
```

```python
import jax
import jax.numpy as jnp
from jax import lax
from jax.experimental import pallas as pl
from jax.experimental.pallas import tpu as pltpu
from jax.sharding import PartitionSpec as P

WIN = 128
LANES = 128
EDGE = 2
HIGH = lax.Precision.HIGHEST
ROWS = 8
DEPTH = 6 * ROWS


def features_kernel(window_ref, params_ref, hidden_ref, shifted):
    chans = hidden_ref.shape[0]
    tile = window_ref.shape[2]
    width = tile // LANES
    lat = window_ref.shape[1]
    span = WIN * LANES
    total = span + 2 * EDGE * LANES
    lane = lax.broadcasted_iota(jnp.int32, (ROWS, tile), 1) % LANES
    zeros_edge = jnp.zeros((ROWS, EDGE * LANES), jnp.float32)
    for a in range(3):
        shifted[a, :, 0 : EDGE * LANES] = zeros_edge
        shifted[a, :, total - EDGE * LANES : total] = zeros_edge
        shifted[a, :, total - (EDGE + 1) * LANES : total - EDGE * LANES] = zeros_edge[:, :LANES]
    for part in range(window_ref.shape[0]):
        cells = window_ref[part].astype(jnp.float32)
        cells = jnp.concatenate([cells, cells], axis=0)
        at = EDGE * LANES + part * tile
        views = (
            jnp.where(lane == 0, 0.0, pltpu.roll(cells, 1, 1)),
            cells,
            jnp.where(lane == LANES - 1, 0.0, pltpu.roll(cells, tile - 1, 1)),
        )
        for a, view in enumerate(views):
            shifted[a, 0:lat, at : at + tile] = view[0:lat]
            shifted[a, lat : 2 * lat, at - LANES : at + tile - LANES] = view[lat : 2 * lat]

    def patches(start, size):
        return jnp.concatenate(
            [shifted[a, :, pl.ds(start + 2 * b * LANES, size)] for a in range(3) for b in range(2)],
            axis=0,
        )

    depth = DEPTH
    columns = params_ref[...].T
    w = columns[0:chans, 0:depth]
    w_bf = w.astype(jnp.bfloat16)
    gain = jnp.broadcast_to(columns[0:chans, depth : depth + 1], (chans, LANES))
    shift = jnp.broadcast_to(columns[0:chans, depth + 1 : depth + 2], (chans, LANES))
    count = float(span)
    first_cell = (EDGE - 1) * LANES
    xbar = jnp.sum(patches(first_cell, span), axis=1, keepdims=True) * (1.0 / count)
    same = jnp.zeros((depth, depth), jnp.float32)
    cross = same
    chunk = 2048
    dims = (((1,), (1,)), ((), ()))
    for step in range(span // chunk):
        centred = patches(first_cell + step * chunk, chunk) - xbar
        high = centred.astype(jnp.bfloat16)
        low = (centred - high.astype(jnp.float32)).astype(jnp.bfloat16)
        same = same + lax.dot_general(high, high, dims, preferred_element_type=jnp.float32)
        cross = cross + lax.dot_general(high, low, dims, preferred_element_type=jnp.float32)
    spread = (same + 2.0 * cross) * (1.0 / count)
    chan_mean = jnp.dot(
        w, jnp.broadcast_to(xbar, (depth, LANES)), precision=HIGH, preferred_element_type=jnp.float32
    )
    quad = jnp.dot(w, spread, precision=HIGH, preferred_element_type=jnp.float32) * w
    chan_var = jnp.sum(quad, axis=1, keepdims=True)
    of_row = (lax.broadcasted_iota(jnp.int32, (chans, chans), 0) * 6554) >> 16
    of_col = (lax.broadcasted_iota(jnp.int32, (chans, chans), 1) * 6554) >> 16
    member = (of_row == of_col).astype(jnp.float32)
    mean = jnp.dot(member, chan_mean, precision=HIGH, preferred_element_type=jnp.float32) * 0.1
    off = chan_mean - mean
    var = jnp.dot(member, chan_var + off * off, precision=HIGH, preferred_element_type=jnp.float32) * 0.1
    scale = 0.5 * gain / jnp.sqrt(var + 1e-05)
    base = 0.5 * shift - mean * scale

    phase = lax.rem(lax.axis_index("col") + 30, 4)
    first, last = phase == 0, phase == 3
    scale2 = jnp.concatenate([scale, scale], axis=1)
    base2 = jnp.concatenate([base, base], axis=1)
    pairs = (width + 2) // 2
    for pair in range(pairs):
        start = phase * tile + pair * 2 * LANES
        cells = jnp.concatenate(
            [
                shifted[a, :, pl.ds(pl.multiple_of(start + 2 * b * LANES, LANES), 2 * LANES)]
                for a in range(3)
                for b in range(2)
            ],
            axis=0,
        ).astype(jnp.bfloat16)
        feat = jnp.dot(w_bf, cells, preferred_element_type=jnp.float32)
        half = feat * scale2 + base2
        act = half * jnp.tanh(half) + half
        if pair == 0:
            act = jnp.concatenate([jnp.where(first, 0.0, act[:, :LANES]), act[:, LANES:]], axis=1)
        if pair == pairs - 1:
            act = jnp.concatenate([act[:, :LANES], jnp.where(last, 0.0, act[:, LANES:])], axis=1)
        hidden_ref[:, pair * 2 * LANES : (pair + 1) * 2 * LANES] = act.astype(jnp.bfloat16)


def features(window, params, chans):
    width = window.shape[2] // LANES
    return pl.pallas_call(
        features_kernel,
        out_shape=jax.ShapeDtypeStruct((chans, (width + 2) * LANES), jnp.bfloat16),
        in_specs=[pl.BlockSpec(memory_space=pltpu.VMEM)] * 2,
        out_specs=pl.BlockSpec(memory_space=pltpu.VMEM),
        scratch_shapes=[pltpu.VMEM((3, ROWS, (WIN + 2 * EDGE) * LANES), jnp.float32)],
        compiler_params=pltpu.CompilerParams(vmem_limit_bytes=16 * 2**20),
        name="features",
    )(in_vmem(window), in_vmem(params))


KPAD = 512
SPARE = 32
COLS = 4
HALF_COLS = 16
BLOCK = 80
VMEM = pl.BlockSpec(memory_space=pltpu.VMEM)
SMEM = pl.BlockSpec(memory_space=pltpu.SMEM)


def position():
    col = lax.axis_index("col")
    return lax.rem(col, 2), lax.rem(lax.div(col, 2), 4), lax.div(col, 8)


def in_vmem(value):
    return pltpu.with_memory_space_constraint(value, pltpu.VMEM)


def split_float(value):
    high = value.astype(jnp.bfloat16).astype(jnp.float32)
    return high, value - high


LOW = pltpu.CompilerParams(vmem_limit_bytes=8 * 2**20)


def prepare_kernel(step_ref, *rest):
    w_conv_ref, third_ref, latent_ref, one_ref, two_ref, w_in_ref = rest[13:19]
    gain_ref, shift_ref = rest[19:21]
    rows, sems = rest[21:]
    copies = [pltpu.make_async_copy(rest[i], rest[13 + i], sems.at[i]) for i in range(8)]
    for copy in copies:
        copy.start()
    mine_ref, theirs_ref, own_ref, part_ref, params_ref = rest[8:13]
    core, _, _ = position()
    shard, chans = w_conv_ref.shape[1:]
    half, temb_half = chans // 2, third_ref.shape[1] // 2
    rows[...] = jnp.zeros(rows.shape, jnp.float32)
    params_ref[...] = jnp.zeros(params_ref.shape, jnp.float32)
    lane = lax.broadcasted_iota(jnp.int32, (8, chans), 1)
    k = jnp.where(lane < half, lane, lane - half).astype(jnp.float32)
    freq = jnp.exp(-jnp.log(jnp.float32(10000.0)) * k / jnp.float32(half))
    for copy in copies:
        copy.wait()
    own_ref[...] = latent_ref[...].astype(jnp.bfloat16)
    for h in range(2):
        for a in range(3):
            for b in range(3):
                at = a * KPAD + b * half
                rows[h, 0:shard, at : at + half] = w_conv_ref[
                    3 * a + b, :, h * half : (h + 1) * half
                ].astype(jnp.float32)
        rows[h, 0:shard, 3 * KPAD :] = third_ref[:, h * temb_half : (h + 1) * temb_half].astype(
            jnp.float32
        )
    mine_ref[...] = rows[core].astype(jnp.bfloat16)
    theirs_ref[...] = rows[1 - core].astype(jnp.bfloat16)
    lat, depth = w_in_ref.shape[1], DEPTH
    for tap in range(w_in_ref.shape[0]):
        at = tap // 3 * 2 * ROWS + tap % 3 * lat
        params_ref[at : at + lat, 0:chans] = w_in_ref[tap].astype(jnp.float32)
    params_ref[depth : depth + 1, 0:chans] = gain_ref[...].reshape(1, chans)
    params_ref[depth + 1 : depth + 2, 0:chans] = shift_ref[...].reshape(1, chans)
    angle = step_ref[0].astype(jnp.float32) * freq
    emb = jnp.where(lane < half, jnp.cos(angle), jnp.sin(angle))
    first = lax.dot_general(
        emb,
        one_ref[...].astype(jnp.float32),
        (((1,), (1,)), ((), ())),
        precision=HIGH,
        preferred_element_type=jnp.float32,
    )
    first = (first / (1.0 + jnp.exp(-first))).astype(jnp.bfloat16)
    second = jnp.dot(first, two_ref[...], preferred_element_type=jnp.float32)
    high, low = split_float(second)
    row = lax.broadcasted_iota(jnp.int32, second.shape, 0)
    part_ref[...] = jnp.where(row == 0, high, jnp.where(row == 1, low, 0.0))


def prepare(step, w_conv, third, latent, w_one, w_two, w_in, gain, shift):
    wide = 3 * KPAD + third.shape[1] // 2
    inputs = (w_conv, third, latent, w_one, w_two, w_in, gain, shift)
    inputs = [pltpu.with_memory_space_constraint(v, pltpu.HBM) for v in inputs]
    return pl.pallas_call(
        prepare_kernel,
        out_shape=(
            jax.ShapeDtypeStruct((16, wide), jnp.bfloat16),
            jax.ShapeDtypeStruct((16, wide), jnp.bfloat16),
            jax.ShapeDtypeStruct(latent.shape, jnp.bfloat16),
            jax.ShapeDtypeStruct((8, w_two.shape[1]), jnp.float32),
            jax.ShapeDtypeStruct((LANES, 3 * LANES), jnp.float32),
        ),
        in_specs=[SMEM] + [pl.BlockSpec(memory_space=pltpu.HBM)] * len(inputs),
        out_specs=(VMEM,) * 5,
        scratch_shapes=[pltpu.VMEM(v.shape, v.dtype) for v in inputs]
        + [pltpu.VMEM((2, 16, wide), jnp.float32), pltpu.SemaphoreType.DMA((len(inputs),))],
        compiler_params=LOW,
        name="prepare",
    )(step, *inputs)


def pair_kernel(mine_ref, got_ref, time_ref, out_ref, rows):
    core, _, _ = position()
    shard = 10
    temb = time_ref.shape[1]
    mine = mine_ref[...].astype(jnp.float32)
    got = got_ref[...].astype(jnp.float32)
    rows[0:16, :] = jnp.where(core == 0, mine, got)
    rows[shard : shard + 16, :] = jnp.where(core == 0, got, mine)
    rows[2 * shard : 2 * shard + 8, 0:temb] = time_ref[...]
    out_ref[...] = rows[0:24, :].astype(jnp.bfloat16)


def pair_up(mine, got, part):
    wide = mine.shape[1]
    return pl.pallas_call(
        pair_kernel,
        out_shape=jax.ShapeDtypeStruct((24, wide), jnp.bfloat16),
        in_specs=[VMEM] * 3,
        out_specs=VMEM,
        scratch_shapes=[pltpu.VMEM((32, wide), jnp.float32)],
        compiler_params=LOW,
        name="pair_up",
    )(in_vmem(mine), in_vmem(got), in_vmem(part))


def block_kernel(*rest):
    parts, out_ref, held, rows = rest[:4], rest[4], rest[5], rest[6]
    _, z_lo, _ = position()
    temb = 1280
    total = jnp.zeros((1, temb), jnp.float32)
    for k in range(4):
        part = parts[k][...].astype(jnp.float32)
        total = total + part[20:21, :temb] + part[21:22, :temb]
        held[(z_lo + k) % 4] = part
    for k in range(4):
        rows[20 * k : 20 * k + 24, :] = held[k]
    high, low = split_float(total)
    for q in range(temb // SPARE):
        piece = slice(q * SPARE, (q + 1) * SPARE)
        rows[q : q + 1, KPAD - SPARE : KPAD] = high[:, piece]
        rows[q : q + 1, 2 * KPAD - SPARE : 2 * KPAD] = low[:, piece]
    out_ref[...] = rows[0:BLOCK, :].astype(jnp.bfloat16)


def make_block(parts):
    wide = parts[0].shape[1]
    return pl.pallas_call(
        block_kernel,
        out_shape=jax.ShapeDtypeStruct((BLOCK, wide), jnp.bfloat16),
        in_specs=[VMEM] * 4,
        out_specs=VMEM,
        scratch_shapes=[pltpu.VMEM((4, 24, wide), jnp.float32), pltpu.VMEM((88, wide), jnp.float32)],
        compiler_params=LOW,
        name="make_block",
    )(*[in_vmem(v) for v in parts])


def pick(rows, cols, offset, down):
    source = lax.broadcasted_iota(jnp.int32, (rows, cols), 1 if down else 0)
    target = lax.broadcasted_iota(jnp.int32, (rows, cols), 0 if down else 1)
    return jnp.where(source == target + offset, 1.0, 0.0).astype(jnp.bfloat16)


def strip_kernel(offset_ref, own_ref, beside_ref, out_ref):
    width = own_ref.shape[1]
    chosen = pick(width, 2 * width, offset_ref[0], True)
    for c in range(own_ref.shape[0]):
        both = jnp.concatenate([own_ref[c], beside_ref[c]], axis=0)
        out_ref[c] = jnp.dot(chosen, both, preferred_element_type=jnp.float32).astype(jnp.bfloat16)


def moved_kernel(offset_ref, strip_ref, below_ref, out_ref, stacked, flat):
    lat, width, height = strip_ref.shape
    chosen = pick(2 * height, height, offset_ref[0], False)
    for c in range(lat):
        both = jnp.concatenate([strip_ref[c], below_ref[c]], axis=1)
        stacked[c * width : (c + 1) * width, :] = jnp.dot(
            both, chosen, preferred_element_type=jnp.float32
        )
    for j in range(width):
        flat[0:lat, j * height : (j + 1) * height] = stacked[pl.ds(j, lat, stride=width), :]
    out_ref[0] = flat[0:lat, :].astype(jnp.bfloat16)


def shift_columns(offset, own, beside):
    return pl.pallas_call(
        strip_kernel,
        out_shape=jax.ShapeDtypeStruct(own.shape, own.dtype),
        in_specs=[SMEM] + [VMEM] * 2,
        out_specs=VMEM,
        compiler_params=LOW,
        name="strip",
    )(offset, in_vmem(own), in_vmem(beside))


def shift_rows(offset, strip, below):
    lat, width, height = strip.shape
    return pl.pallas_call(
        moved_kernel,
        out_shape=jax.ShapeDtypeStruct((1, lat, width * height), strip.dtype),
        in_specs=[SMEM] + [VMEM] * 2,
        out_specs=VMEM,
        scratch_shapes=[
            pltpu.VMEM((lat * width, height), jnp.float32),
            pltpu.VMEM((ROWS, width * height), jnp.float32),
        ],
        compiler_params=LOW,
        name="moved",
    )(offset, in_vmem(strip), in_vmem(below))


def conv_kernel(hidden_ref, *rest):
    refs, (out_ref, prod_a, prod_b, wide, staged, line, sems) = rest[:8], rest[8:]
    prods = (prod_a, prod_b)
    core, _, xpos = position()
    chans = hidden_ref.shape[0]
    half = chans // 2
    own = pl.multiple_of(core * half, 16)
    other = pl.multiple_of((1 - core) * half, 16)
    n = COLS * LANES
    temb_half = refs[0].shape[1] - 3 * KPAD
    lane = lax.broadcasted_iota(jnp.int32, (BLOCK, n), 1) % LANES

    def block(side, k, first, last):
        return refs[4 * side + k][0:BLOCK, first:last]

    spare = jnp.zeros((48, LANES), jnp.float32)
    for ref in refs:
        for a in range(2):
            at = (a + 1) * KPAD
            spare = spare + ref[0:48, at - LANES : at].astype(jnp.float32)
    for q in range(2 * temb_half // SPARE):
        line[0:1, q * SPARE : (q + 1) * SPARE] = spare[q : q + 1, LANES - SPARE : LANES]
    second = line[0:1, :]
    s_two = second / (1.0 + jnp.exp(-second))
    s_two = s_two.astype(jnp.bfloat16).astype(jnp.float32)
    s_low, s_high = s_two[:, :temb_half], s_two[:, temb_half:]
    s_sides = (jnp.where(core == 0, s_low, s_high), jnp.where(core == 0, s_high, s_low))
    tvecs = []
    for k in range(4):
        terms = [
            block(side, k, 3 * KPAD, 3 * KPAD + temb_half).astype(jnp.float32) * s_sides[side]
            for side in range(2)
        ]
        tvecs.append(jnp.sum(terms[0] + terms[1], axis=1, keepdims=True))

    def multiply(col, prod):
        right = []
        for rows in (own, other):
            for b in range(3):
                at = (col + b) * LANES
                right.append(hidden_ref[pl.ds(rows, half), at : at + n])
            right.append(jnp.zeros((SPARE, n), jnp.bfloat16))
        right = jnp.concatenate(right, axis=0)
        left = jnp.concatenate(
            [
                jnp.concatenate([block(side, k, a * KPAD, (a + 1) * KPAD) for side in range(2)], axis=1)
                for k in range(4)
                for a in range(3)
            ],
            axis=0,
        )
        prod[...] = jnp.dot(left, right, preferred_element_type=jnp.float32)

    def finish(local, prod):
        for k in range(4):
            at = 3 * k * BLOCK
            low = prod[at : at + BLOCK, :]
            mid = prod[at + BLOCK : at + 2 * BLOCK, :]
            high = prod[at + 2 * BLOCK : at + 3 * BLOCK, :]
            done = (
                mid
                + jnp.where(lane == 0, 0.0, pltpu.roll(low, 1, 1))
                + jnp.where(lane == LANES - 1, 0.0, pltpu.roll(high, n - 1, 1))
                + tvecs[k]
            )
            chan = (xpos + (0, 1, 3, 2)[k]) % 4 * BLOCK
            for j in range(COLS):
                first = chan * HALF_COLS + local + j
                wide[pl.ds(first, BLOCK, stride=HALF_COLS), :] = done[:, j * LANES : (j + 1) * LANES]

    width = out_ref.shape[1]
    tiles, per = width // COLS, HALF_COLS // COLS
    copies = []
    for t in range(tiles + 1):
        if t < tiles:
            multiply(t * COLS, prods[t % 2])
        if t > 0:
            finish((t - 1) % per * COLS, prods[(t - 1) % 2])
            if t % per == 0:
                h = t // per - 1
                parts = 1 if t < tiles else 4
                size = chans // parts
                for part in range(parts):
                    at = part * size
                    cells = wide[at * HALF_COLS : (at + size) * HALF_COLS, :]
                    staged[h, at : at + size] = cells.reshape(size, HALF_COLS, LANES).astype(jnp.bfloat16)
                    copy = pltpu.make_async_copy(
                        staged.at[h, pl.ds(at, size)],
                        out_ref.at[pl.ds(at, size), pl.ds(h * HALF_COLS, HALF_COLS), :],
                        sems.at[len(copies)],
                    )
                    copy.start()
                    copies.append(copy)
    for copy in copies:
        copy.wait()


def conv(hidden, pieces):
    chans, padded = hidden.shape
    width = padded // LANES - 2
    halves = width // HALF_COLS
    return pl.pallas_call(
        conv_kernel,
        out_shape=jax.ShapeDtypeStruct((chans, width, LANES), jnp.bfloat16),
        in_specs=[VMEM] * (1 + len(pieces)),
        out_specs=pl.BlockSpec(memory_space=pl.ANY),
        scratch_shapes=[
            pltpu.VMEM((3 * chans, COLS * LANES), jnp.float32),
            pltpu.VMEM((3 * chans, COLS * LANES), jnp.float32),
            pltpu.VMEM((chans * HALF_COLS, LANES), jnp.float32),
            pltpu.VMEM((halves, chans, HALF_COLS, LANES), jnp.bfloat16),
            pltpu.VMEM((8, 1280), jnp.float32),
            pltpu.SemaphoreType.DMA((halves + 3,)),
        ],
        compiler_params=pltpu.CompilerParams(vmem_limit_bytes=20 * 2**20),
        name="convolve",
    )(in_vmem(hidden), *[in_vmem(v) for v in pieces])


def pairs_of(move):
    pairs = []
    for row in range(8):
        for col in range(32):
            y, z_hi, x, z_lo, core = row // 2, row % 2, col // 8, col // 2 % 4, col % 2
            z = z_hi * 4 + z_lo
            y, z, x, core = move(y, z, x, core)
            y, z, x = y % 4, z % 8, x % 4
            pairs.append((row * 32 + col, (y * 2 + z // 4) * 32 + x * 8 + z % 4 * 2 + core))
    return pairs


def send(value, move):
    return lax.ppermute(value, ("row", "col"), pairs_of(move))


def fetch_grid(value, rows, cols):
    pairs = [
        ((r + rows) % 8 * 32 + (c + cols) % 32, r * 32 + c) for r in range(8) for c in range(32)
    ]
    return lax.ppermute(value, ("row", "col"), pairs)


def swap_core(value):
    return send(value, lambda y, z, x, core: (y, z, x, 1 - core))


def from_z(value, steps):
    return send(value, lambda y, z, x, core: (y, z - steps, x, core))


def from_x(value, steps):
    return send(value, lambda y, z, x, core: (y, z, x - steps, core))


WINDOW_GROUPS = [[r * 32 + (4 * p + 2 + k) % 32 for k in range(4)] for r in range(8) for p in range(8)]


def body(
    latent,
    row_offset,
    col_offset,
    timestep,
    w_in,
    norm_gain,
    norm_shift,
    w_conv,
    w_time1,
    w_time2,
    w_time3,
):
    chans = w_in.shape[1]
    mine, theirs, own, part, params = prepare(
        timestep,
        w_conv,
        w_time3.T,
        latent,
        w_time1.T,
        w_time2,
        w_in.transpose(0, 2, 1),
        norm_gain,
        norm_shift,
    )
    beside = fetch_grid(own, 0, 1)
    got = swap_core(theirs)
    got, beside = lax.optimization_barrier((got, beside))
    zrow = pair_up(mine, got, part)
    near = [zrow, from_z(zrow, 1), from_z(zrow, 2), from_z(zrow, -1)]
    strip = shift_columns(col_offset, own, beside)
    below = fetch_grid(strip, 1, 0)
    near, below = lax.optimization_barrier((near, below))
    block = make_block(near)
    after, before, across = from_x(block, 1), from_x(block, -1), from_x(block, 2)

    moved = shift_rows(row_offset, strip, below)
    window = lax.all_gather(
        moved, ("row", "col"), axis_index_groups=WINDOW_GROUPS, axis=0, tiled=True
    )
    hidden = features(window, params, chans)
    far = lax.optimization_barrier((after, before, across, hidden))
    after, before, across, hidden = far
    pieces = [block, after, before, across]
    pieces = pieces + [swap_core(v) for v in pieces]
    return conv(hidden, pieces)


def solution(mesh):
    return jax.shard_map(
        body,
        mesh=mesh,
        in_specs=(
            P(None, "col", "row"),
            P(),
            P(),
            P(),
            P(),
            P(),
            P(),
            P(None, "col", None),
            P(None, "col"),
            P("col", None),
            P(None, "col"),
        ),
        out_specs=P(None, "col", "row"),
        check_vma=False,
    )
```
